32 devices in a mesh: ax: 8 (over y, x, core), ev: 4 (over z).
Axes of the slice: x: 2, y: 2, z: 4, core: 2. Of those that a mesh axis runs over, the one named last changes fastest.
Arguments:
- home: int32 [16384, 1], P(('ax', 'ev')), may hold values from 0 to 7; in each aligned block of 512 rows (0 to 511, 512 to 1023, ...) at most 256 rows name the same one
- tiles: int32 [16384, 8], P(('ax', 'ev')), may hold values from 0 to 24575, as said below
- classes: int32 [16384, 8], P(('ax', 'ev')), may hold values from 0 to 7
- tof_bins: int32 [16384, 128], P(('ax', 'ev')), may hold values from 0 to 15
- subset: int32 [16384, 128], P(('ax', 'ev')), may hold values 0 or 1
- correction: float32 [16384, 128], P(('ax', 'ev')), may hold values from 0.2 to 1
- background: float32 [16384, 128], P(('ax', 'ev')), may hold values from 0.05 to 0.5
- image: float32 [65536, 128], P('ax'), may hold values from 0.3 to 3
- sensitivity: float32 [65536, 128], P(('ax', 'ev')), may hold values from 1 to 4
- system_table: bfloat16 [128, 1024], replicated, may hold values from 0.00049 to 0.121
Outputs:
- new_image: float32 [65536, 128], P(('ax', 'ev'))
The draws below stay inside these ranges and needn't reach their ends.
Inputs may be any that keep to these rules, and one draw needn't show every extreme that they name: Among the rows of one device, at most 256 bundles name the same home slab, a bound that some block reaches of them. `tiles`: entries k < 2 lie in the slabs home-1 or home (below 16384), entries k >= 6 in the slabs home or home+1 (at least 8192), all others in the home slab.
All inputs are finite; a program needn't handle non-finite values. No bound on the sum of `subset` on one device may be relied on, other than what follows from the above.
Results may differ from the reference program's by a relative error of at most 0.0019.
Values may be sent and summed in bfloat16 or wider, within the bound.
A program may use at most 128 MiB of HBM per device.

```python
import math
import jax
import jax.numpy as jnp
import numpy as np
from jax import lax

TILE = 128
K = 8
NC = 8
NTOF = 16
BUN_DEV = 512
TILES_DEV = 8192
TILES = 65536
BUNDLES = 16384
CAP = 256
N_AX = 8


def draw_tiles(key, part):
    key = jax.random.fold_in(key, 11)
    first, second, third = jax.random.split(key, 3)
    edge = K // 4
    lower = jax.random.randint(first, (BUNDLES, edge), 0, 2 * TILES_DEV)
    middle = jax.random.randint(second, (BUNDLES, K - 2 * edge), TILES_DEV, 2 * TILES_DEV)
    upper = jax.random.randint(third, (BUNDLES, edge), TILES_DEV, 3 * TILES_DEV)
    return jnp.concatenate([lower, middle, upper], 1).astype(jnp.int32)


def log_between(key, shape, low, high):
    level = jax.random.uniform(key, shape, jnp.float32, jnp.log(low), jnp.log(high))
    return jnp.exp(level)


def draw_image(key, part):
    key = jax.random.fold_in(key, 23)
    first, second = jax.random.split(key)
    shape = (TILES, TILE)
    coin = jax.random.randint(first, shape, 0, 2)
    level = jnp.where(coin == 1, 2.0, 0.5).astype(jnp.float32)
    jitter = log_between(second, shape, 0.8, 1.25)
    return (level * jitter).astype(jnp.float32)


def draw_system_table(key, part):
    key = jax.random.fold_in(key, 31)
    first, second, third = jax.random.split(key, 3)
    shape = (TILE, NC * TILE)
    band = jax.random.randint(first, shape, 0, 16) == 0
    strong = log_between(second, shape, 0.04, 0.12)
    faint = log_between(third, shape, 0.0005, 0.003)
    return jnp.where(band, strong, faint).astype(jnp.bfloat16)


def plant(result, own_key, low, largest):
    extent = result.shape
    index_at = [jax.random.randint(jax.random.fold_in(own_key, axis), (), 0, extent[axis]) for axis in range(len(extent))]
    result = result.at[tuple(index_at)].set(low)
    longest = extent.index(max(extent))
    index_at[longest] = (index_at[longest] + 1) % extent[longest]
    return result.at[tuple(index_at)].set(largest)


def shard_levels(key, extent, cuts, low, top_value):
    loudness, own = 1.0, jax.random.fold_in(key, 6)
    for dim, blocks in cuts:
        steps = jnp.exp(jax.random.uniform(jax.random.fold_in(own, dim), (blocks,), jnp.float32, low / len(cuts), top_value / len(cuts)))
        loudness = loudness * jnp.repeat(steps, extent[dim] // blocks).reshape([-1 if axis == dim else 1 for axis in range(len(extent))])
    return loudness


def deal_out(key, own, number, rows, amount, top, most, skew):
    ranking = jax.random.permutation(key, amount)
    packed, usual = load_shares(amount, rows * top, most, skew, True), load_shares(amount, rows * top, most, skew, False)
    places = jnp.arange(amount)

    def named(tallies, turn):
        used = int((tallies > 0).sum())
        fixed = max(1, used // 4)
        passed = fixed + (places - fixed + turn * (used - fixed)) % max(1, amount - fixed)
        return jnp.zeros((amount,), jnp.int32).at[ranking[jnp.where(places < fixed, places, passed)]].set(jnp.asarray(tallies, jnp.int32))

    tallies = jnp.where(number % 4 == 0, named(packed, number // 4), named(usual, number - number // 4 - 1))
    mixed = jax.random.permutation(jax.random.fold_in(own, 3), amount)
    donor, sink = mixed[0:amount // 2 * 2:2], mixed[1:amount // 2 * 2:2]
    margin = jnp.minimum(tallies[donor] - 1, most - tallies[sink]) // 2
    margin = jnp.where((donor == ranking[0]) | (sink == ranking[0]) | (tallies[sink] == 0), 0, jnp.maximum(margin, 0))
    passed = jax.random.randint(jax.random.fold_in(own, 4), (amount // 2,), 0, 1 << 20) % (margin + 1)
    tallies = tallies.at[donor].add(-passed).at[sink].add(passed)
    labels = jnp.searchsorted(jnp.cumsum(tallies), jnp.arange(rows * top), side="right").astype(jnp.int32)
    listing = labels.reshape(top, rows).T
    listing = listing[jax.random.permutation(jax.random.fold_in(own, 1), rows)]
    turn = jax.random.randint(jax.random.fold_in(own, 2), (rows, 1), 0, top)
    return jnp.take_along_axis(listing, (jnp.arange(top)[None, :] + turn) % top, axis=1)


def load_shares(amount, total, reach, slope, full):
    loads = [(1 << 20) // math.isqrt(grade ** slope) + 1 for grade in range(1, amount + 1)]
    largest = reach if full else min(reach, max(-(-total // amount), total * loads[0] // sum(loads)))
    least = 1 if total - largest >= amount - 1 else 0
    counts, rest = [largest] + [least] * (amount - 1), total - largest - least * (amount - 1)
    while rest > 0:
        movable = [i for i in range(1, amount) if counts[i] < largest] or [i for i in range(1, amount) if counts[i] < reach]
        whole, remaining = sum([loads[i] for i in movable]), rest
        for i in movable:
            more = min(reach - counts[i], max(1, remaining * loads[i] // whole), rest)
            counts[i] = counts[i] + more
            rest = rest - more
    return np.array(counts)


def setup_inputs(seed: int = 0) -> dict:
    keys = jax.random.split(jax.random.key(seed), 11)
    home_keys = jax.random.split(jax.random.fold_in(keys[0], 1), BUNDLES // BUN_DEV)
    home_turns = jax.random.permutation(jax.random.fold_in(keys[0], 3), BUNDLES // BUN_DEV)
    home = jax.vmap(lambda own, number: deal_out(jax.random.fold_in(keys[0], 2), own, number, BUN_DEV, N_AX, 1, CAP, 2))(home_keys, home_turns).reshape((BUNDLES, 1))
    tiles = draw_tiles(jax.random.fold_in(keys[10], 71), 0)
    classes = plant(jax.random.randint(keys[2], (BUNDLES, K), 0, NC), jax.random.fold_in(keys[2], 1), 0, NC - 1).astype(jnp.int32)
    tof_bins = plant(jax.random.randint(keys[3], (BUNDLES, TILE), 0, NTOF), jax.random.fold_in(keys[3], 1), 0, NTOF - 1).astype(jnp.int32)
    subset = plant((jax.random.randint(keys[4], (BUNDLES, TILE), 0, 2) < 1).astype(jnp.int32), jax.random.fold_in(keys[4], 1), 0, 1)
    correction = jnp.clip(jnp.exp(math.log(1.0) - 1.609438 * jax.random.uniform(keys[5], (BUNDLES, TILE), jnp.float32) ** shard_levels(keys[5], (BUNDLES, TILE), ((0, 32),), -0.2, 0.2)), 0.2, 1.0)
    background = jnp.clip(jnp.exp(math.log(0.5) - 2.3025851 * jax.random.uniform(keys[6], (BUNDLES, TILE), jnp.float32) ** shard_levels(keys[6], (BUNDLES, TILE), ((0, 32),), -0.2, 0.2)), 0.05, 0.5)
    image = draw_image(jax.random.fold_in(keys[10], 71), 0)
    sensitivity = jnp.clip(jnp.exp(math.log(4.0) - 1.3862944 * jax.random.uniform(keys[8], (TILES, TILE), jnp.float32) ** shard_levels(keys[8], (TILES, TILE), ((0, 32),), -0.2, 0.2)), 1.0, 4.0)
    system_table = draw_system_table(jax.random.fold_in(keys[10], 71), 0)
    return dict(home=home, tiles=tiles, classes=classes, tof_bins=tof_bins, subset=subset, correction=correction, background=background, image=image, sensitivity=sensitivity, system_table=system_table)


spread = 1.0


def kernel_weights(tof_bins, count):
    pos = (tof_bins.astype(jnp.float32) + 0.5) * (count / NTOF)
    centre = jnp.arange(count, dtype=jnp.float32) + 0.5
    return jnp.exp(-(pos[:, None, :] - centre[None, :, None]) ** 2 / (2.0 * spread * spread))


def reference(home, tiles, classes, tof_bins, subset, correction, background, image, sensitivity, system_table):
    total = image.shape[0]
    tile = image.shape[1]
    count = tiles.shape[1]
    kinds = system_table.shape[1] // tile
    padded = jnp.concatenate([image.astype(jnp.bfloat16), jnp.zeros((1, tile), jnp.bfloat16)], 0)
    table = system_table.astype(jnp.float32)
    weight = subset.astype(jnp.float32) * correction
    place = (home - 1) * TILES_DEV + tiles
    valid = (place >= 0) & (place < total)
    place = jnp.where(valid, place, total).astype(jnp.int32)
    bundles = home.shape[0]
    group = math.gcd(bundles, 2048)
    turns = bundles // group
    xs = (place.reshape(turns, group, count), classes.reshape(turns, group, count),
          tof_bins.reshape(turns, group, tile), weight.reshape(turns, group, tile),
          background.reshape(turns, group, tile))

    def step(carry, block):
        index, kind, bins, wgt, bgr = block
        idx = index.reshape(-1)
        cls = kind.reshape(-1)
        gathered = padded[idx].astype(jnp.float32)
        spread_all = jnp.dot(gathered, table, preferred_element_type=jnp.float32, precision=lax.Precision.HIGHEST)
        select = (cls[:, None] == jnp.arange(kinds)[None, :]).astype(jnp.float32)
        forward = jnp.sum(spread_all.reshape(-1, kinds, tile) * select[:, :, None], 1).reshape(group, count, tile)
        kern = kernel_weights(bins, count)
        proj = jnp.sum(kern * forward, 1)
        ratio = wgt / (wgt * proj + bgr)
        back_terms = (kern * ratio[:, None, :]).astype(jnp.bfloat16).astype(jnp.float32)
        spread_back = (back_terms.reshape(-1, 1, tile) * select[:, :, None]).reshape(-1, kinds * tile)
        back = lax.dot_general(spread_back, table, (((1,), (1,)), ((), ())),
                               preferred_element_type=jnp.float32, precision=lax.Precision.HIGHEST)
        return carry.at[idx].add(back), None

    back_image, _ = lax.scan(step, jnp.zeros((total + 1, tile), jnp.float32), xs)
    return image * back_image[:total] / sensitivity
```

```python
import functools
import math

import jax
import jax.numpy as jnp
from jax import lax
from jax.experimental import pallas as pl
from jax.experimental.pallas import tpu as pltpu
from jax.sharding import PartitionSpec as P

NTOF = 16
LEVELS = 64
GROUP = 256
MESH = pl.DeviceIdType.MESH
VMEM_LIMIT = 60 * 1024 * 1024


def neighbours(me):
    odd = me % 2
    return odd, me + 1 - 2 * odd, me - 1 + 2 * odd


def exchange_kernel(
    peers,
    shards,
    home,
    tiles,
    classes,
    bins,
    subset,
    corr,
    bg,
    image,
    got,
    places,
    near,
    far,
    data,
    packed,
    listed_out,
    first,
    whole,
    low_first,
    low_whole,
    send,
    recv,
    local,
):
    count, rows = tiles.shape
    tile = bins.shape[1]
    slab = image.shape[0]
    cap = packed.shape[1]
    half = slab // 2
    part = half // 2
    chunk = 256
    me = lax.axis_index("ax")
    ev = lax.axis_index("ev")
    odd, beside, across = neighbours(me)
    has_far = jnp.logical_and(across >= 0, across < peers)
    side = ev % 2
    mate = ev + 1 - 2 * side
    start = pl.multiple_of(side * half, half)
    pieces = [pl.ds(start + c * part, part) for c in range(2)]
    load_first = pltpu.make_async_copy(image.at[pl.ds(start, half)], first, local.at[0])
    load_whole = pltpu.make_async_copy(image, whole, local.at[1])
    load_first.start()
    load_whole.start()
    barrier = pltpu.get_barrier_semaphore()
    for d in range(1, peers):
        pl.semaphore_signal(barrier, inc=1, device_id=((me + d) % peers, ev), device_id_type=MESH)
    for d in range(1, shards):
        pl.semaphore_signal(barrier, inc=1, device_id=(me, (ev + d) % shards), device_id_type=MESH)

    def remote(src, dst, which, device):
        return pltpu.make_async_remote_copy(
            src_ref=src,
            dst_ref=dst,
            send_sem=send.at[which],
            recv_sem=recv.at[which],
            device_id=device,
            device_id_type=MESH,
        )

    load_first.wait()

    @pl.loop(0, half // chunk)
    def _(i):
        at = pl.ds(pl.multiple_of(i * chunk, chunk), chunk)
        low_first[at, :] = first[at, :].astype(jnp.bfloat16)

    pl.semaphore_wait(barrier, peers + shards - 2)
    far_copies = [
        remote(low_first.at[pl.ds(c * part, part)], far.at[pieces[c]], 2 * c, (across, ev))
        for c in range(2)
    ]
    shares = [remote(far.at[pieces[c]], far.at[pieces[c]], 3 + c, (me, mate)) for c in range(2)]

    @pl.when(has_far)
    def _():
        for copy in far_copies:
            copy.start()

    target = home[...]
    onehot = (
        lax.broadcasted_iota(jnp.int32, (peers, rows), 0) == target
    ).astype(jnp.float32)
    tri = (
        lax.broadcasted_iota(jnp.int32, (rows, rows), 0)
        < lax.broadcasted_iota(jnp.int32, (rows, rows), 1)
    ).astype(jnp.float32).astype(jnp.bfloat16)
    before = jnp.dot(onehot.astype(jnp.bfloat16), tri, preferred_element_type=jnp.float32)
    rank = jnp.sum(before * onehot, axis=0, keepdims=True).astype(jnp.int32)
    place = target * cap + rank
    data[:, 0:tile] = (subset[...].astype(jnp.float32) * corr[...]).astype(jnp.bfloat16)
    data[:, tile : 2 * tile] = bg[...].astype(jnp.bfloat16)
    data[:, 2 * tile : 3 * tile] = bins[...].astype(jnp.float32).astype(jnp.bfloat16)
    which = lax.broadcasted_iota(jnp.int32, (count, 128), 1)
    own = lax.broadcasted_iota(jnp.int32, (count, 128), 0)
    refs = jnp.zeros((rows, 128), jnp.float32)
    listed = tiles[...]
    for turn, part in enumerate((listed >> 8, listed & 255, classes[...])):
        spot = (which == own + turn * count).astype(jnp.float32).astype(jnp.bfloat16)
        refs += lax.dot_general(
            part.astype(jnp.float32).astype(jnp.bfloat16),
            spot,
            (((0,), (0,)), ((), ())),
            preferred_element_type=jnp.float32,
        )
    data[:, 3 * tile :] = refs.astype(jnp.bfloat16)
    slot = lax.broadcasted_iota(jnp.int32, (cap, rows), 0)
    total = jnp.sum(onehot, axis=1, keepdims=True).astype(jnp.int32)
    high_part = (listed >> 8).astype(jnp.float32).astype(jnp.bfloat16)
    low_part = (listed & 255).astype(jnp.float32).astype(jnp.bfloat16)
    for p in range(peers):
        listed_out[p, count : 2 * count, :] = jnp.broadcast_to(total[p : p + 1, :], (count, cap))

    @pl.loop(0, peers)
    def _(p):
        put = (place - p * cap == slot).astype(jnp.float32).astype(jnp.bfloat16)
        packed[p] = jnp.dot(put, data[...], preferred_element_type=jnp.float32).astype(
            jnp.bfloat16
        )
        across_rows = (((1,), (1,)), ((), ()))
        high = lax.dot_general(high_part, put, across_rows, preferred_element_type=jnp.float32)
        base = lax.dot_general(low_part, put, across_rows, preferred_element_type=jnp.float32)
        filled = listed_out[p, count : 2 * count, :]
        lane = lax.broadcasted_iota(jnp.int32, (count, cap), 1)
        listed_out[p, 0:count, :] = jnp.where(
            lane < filled, (high * 256.0 + base).astype(jnp.int32), slab
        )

    load_whole.wait()

    @pl.loop(0, slab // chunk)
    def _(i):
        at = pl.ds(pl.multiple_of(i * chunk, chunk), chunk)
        low_whole[at, :] = whole[at, :].astype(jnp.bfloat16)

    @pl.when(has_far)
    def _():
        far_copies[0].wait_recv()
        shares[0].start()

    others = []
    for d in range(1, peers):
        goal = (me + d) % peers
        others.append(remote(packed.at[goal], got.at[me], shards + d, (goal, ev)))
        others.append(
            remote(listed_out.at[goal], places.at[me], peers + shards + d, (goal, ev))
        )
    others.append(remote(low_whole, near, 1, (beside, ev)))
    for copy in others:
        copy.start()
    keep = pltpu.make_async_copy(packed.at[me], got.at[me], local.at[2])
    keep.start()
    keep_list = pltpu.make_async_copy(listed_out.at[me], places.at[me], local.at[3])
    keep_list.start()

    @pl.when(has_far)
    def _():
        far_copies[1].wait_recv()
        shares[1].start()

    keep.wait()
    keep_list.wait()
    for copy in others:
        copy.wait()

    @pl.when(has_far)
    def _():
        for copy in far_copies:
            copy.wait_send()
        for copy in shares:
            copy.wait()


def project_kernel(
    peers,
    cap,
    group,
    flags,
    tiles,
    got,
    image,
    near,
    far,
    table,
    codes_out,
    units_out,
    own_out,
    win,
    acc_a,
    acc_b,
    acc_c,
    acc_d,
    stage,
    codes,
    units,
    gath,
    back,
    sems,
):
    slab = image.shape[0]
    tile = image.shape[1]
    odd, has_far = flags[0], flags[1]
    kinds = table.shape[1] // tile
    count = tiles.shape[1] // 2
    loads = [
        pltpu.make_async_copy(image, win.at[pl.ds(slab, slab)], sems.at[0]),
        pltpu.make_async_copy(near, stage.at[0], sems.at[1]),
        pltpu.make_async_copy(far, stage.at[1], sems.at[2]),
    ]
    for copy in loads:
        copy.start()
    chunk = 256

    @pl.loop(0, 2 * slab // chunk)
    def _(i):
        at = pl.ds(pl.multiple_of(i * chunk, chunk), chunk)
        for acc in (acc_a, acc_b, acc_c, acc_d):
            acc[at, :] = jnp.zeros((chunk, tile), jnp.float32)

    for copy in loads:
        copy.wait()

    @pl.loop(0, slab // chunk)
    def _(i):
        at = pl.ds(pl.multiple_of(i * chunk, chunk), chunk)
        beside = pl.ds(pl.multiple_of(2 * slab * (1 - odd) + i * chunk, chunk), chunk)
        across = pl.ds(pl.multiple_of(2 * slab * odd + i * chunk, chunk), chunk)
        win[beside, :] = stage[0, at, :].astype(jnp.float32)
        win[across, :] = jnp.where(has_far > 0, stage[1, at, :].astype(jnp.float32), 0.0)

    chains = (
        (acc_a, 0),
        (acc_b, 0),
        (acc_a, 0),
        (acc_b, 0),
        (acc_c, slab),
        (acc_d, slab),
        (acc_c, slab),
        (acc_d, slab),
    )
    order = (0, 1, 4, 5, 2, 3, 6, 7)

    def block(p, first, steps):
        base = p * cap + first

        @pl.loop(0, steps)
        def _(t):
            for b in range(8):
                for k in range(count):
                    idx = tiles[p, k, first + t * 8 + b]
                    gath[pl.ds(k * group + t * 8 + b, 1), :] = win[pl.ds(idx, 1), :]

        at = pl.ds(pl.multiple_of(base, group), group)
        pos = (got[at, 2 * tile : 3 * tile].astype(jnp.float32) + 0.5) * (count / NTOF)
        wgt = got[at, 0:tile].astype(jnp.float32)
        bgr = got[at, tile : 2 * tile].astype(jnp.float32)
        bgr = jnp.where(bgr > 0, bgr, 1.0)
        refs = got[at, 3 * tile : 4 * tile].astype(jnp.float32)
        proj = jnp.zeros((group, tile), jnp.float32)
        kinds_of = []
        kern = []
        for k in range(count):
            kind = jnp.broadcast_to(refs[:, 2 * count + k : 2 * count + k + 1], (group, tile))
            rows = gath[k * group : (k + 1) * group, :].astype(jnp.bfloat16)
            full = jnp.dot(rows, table[...], preferred_element_type=jnp.float32)
            forward = full[:, 0:tile]
            for c in range(1, kinds):
                forward = jnp.where(kind == c, full[:, c * tile : (c + 1) * tile], forward)
            weight = jnp.exp((pos - (k + 0.5)) ** 2 * -0.5)
            proj += weight * forward
            kinds_of.append(kind)
            kern.append(weight)
        ratio = wgt / (wgt * proj + bgr)
        for k in range(count):
            term = kern[k] * ratio
            spread = jnp.concatenate(
                [jnp.where(kinds_of[k] == c, term, 0.0).astype(jnp.bfloat16) for c in range(kinds)],
                axis=1,
            )
            back[k * group : (k + 1) * group, :] = lax.dot_general(
                spread, table[...], (((1,), (1,)), ((), ())), preferred_element_type=jnp.float32
            )

        @pl.loop(0, steps)
        def _(t):
            for b in range(8):
                for k in order:
                    acc, off = chains[k]
                    idx = tiles[p, k, first + t * 8 + b] - off
                    acc[pl.ds(idx, 1), :] += back[pl.ds(k * group + t * 8 + b, 1), :]

    @pl.loop(0, peers)
    def _(p):
        number = tiles[p, count, 0]

        @pl.loop(0, (number + group - 1) // group)
        def _(i):
            block(p, i * group, (jnp.minimum(number - i * group, group) + 7) // 8)

    @pl.loop(0, slab // LEVELS)
    def _(i):
        at = pl.ds(pl.multiple_of(i * LEVELS, LEVELS), LEVELS)
        above = pl.ds(pl.multiple_of(slab + i * LEVELS, LEVELS), LEVELS)
        below_part = acc_a[at, :] + acc_b[at, :]
        above_part = acc_c[above, :] + acc_d[above, :]
        win[at, :] = (acc_a[above, :] + acc_b[above, :]) + (acc_c[at, :] + acc_d[at, :])
        for turn, part in enumerate(
            (
                jnp.where(odd > 0, below_part, above_part),
                jnp.where(odd > 0, above_part, below_part),
            )
        ):
            code, unit = coded(part)
            codes[turn, at, :] = code
            units[turn, pl.ds(i, 1), :] = unit

    stores = [
        pltpu.make_async_copy(codes, codes_out, sems.at[0]),
        pltpu.make_async_copy(units, units_out, sems.at[1]),
        pltpu.make_async_copy(win.at[pl.ds(0, slab)], own_out, sems.at[2]),
    ]
    for copy in stores:
        copy.start()
    for copy in stores:
        copy.wait()


def coded(part):
    largest = jnp.maximum(jnp.max(jnp.abs(part), axis=0, keepdims=True), 1e-30)
    code = jnp.round(part * (32000.0 / largest)).astype(jnp.int32).astype(jnp.int16)
    return code, largest * (1.0 / 32000.0)


def decoded(code, unit):
    return code.astype(jnp.int32).astype(jnp.float32) * unit


def combine_kernel(
    peers,
    shards,
    codes,
    units,
    own,
    image,
    sens,
    out,
    near_in,
    far_in,
    near_unit,
    far_unit,
    z_in,
    z_unit,
    z_out,
    z_unit_out,
    mine,
    img,
    send,
    recv,
    local,
):
    quarter, tile = sens.shape
    slab = own.shape[0]
    blocks = quarter // LEVELS
    me = lax.axis_index("ax")
    ev = lax.axis_index("ev")
    odd, beside, across = neighbours(me)
    has_far = jnp.logical_and(across >= 0, across < peers)
    piece = pl.ds(pl.multiple_of(ev * quarter, quarter), quarter)
    loads = [
        pltpu.make_async_copy(own, mine, local.at[0]),
        pltpu.make_async_copy(image.at[piece], img, local.at[1]),
    ]
    for copy in loads:
        copy.start()
    barrier = pltpu.get_barrier_semaphore()
    for d in range(1, peers):
        pl.semaphore_signal(barrier, inc=1, device_id=((me + d) % peers, ev), device_id_type=MESH)
    for d in range(1, shards):
        pl.semaphore_signal(barrier, inc=1, device_id=(me, (ev + d) % shards), device_id_type=MESH)
    pl.semaphore_wait(barrier, peers + shards - 2)

    def remote(src, dst, which, device):
        return pltpu.make_async_remote_copy(
            src_ref=src,
            dst_ref=dst,
            send_sem=send.at[which],
            recv_sem=recv.at[which],
            device_id=device,
            device_id_type=MESH,
        )

    turns = [(ev + 1 + j) % shards for j in range(shards)]
    far_copies = [remote(units.at[1], far_unit, 2 * shards, (across, ev))]
    near_copies = [remote(units.at[0], near_unit, 2 * shards + 1, (beside, ev))]
    for j, turn in enumerate(turns):
        at = pl.ds(pl.multiple_of(turn * quarter, quarter), quarter)
        far_copies.append(remote(codes.at[1, at], far_in.at[at], j, (across, ev)))
        near_copies.append(remote(codes.at[0, at], near_in.at[at], shards + j, (beside, ev)))

    @pl.when(has_far)
    def _():
        for copy in far_copies[:3]:
            copy.start()

    for copy in near_copies:
        copy.start()
    for copy in loads:
        copy.wait()
    near_copies[0].wait_recv()

    @pl.when(has_far)
    def _():
        far_copies[0].wait_recv()

    shares = []
    for j, turn in enumerate(turns):
        near_copies[1 + j].wait_recv()

        @pl.when(has_far)
        def _():
            far_copies[1 + j].wait_recv()
            for copy in far_copies[3 + j : 4 + j]:
                copy.start()

        @pl.loop(0, blocks)
        def _(i):
            row = turn * blocks + i
            at = pl.ds(pl.multiple_of(row * LEVELS, LEVELS), LEVELS)
            to = pl.ds(pl.multiple_of(i * LEVELS, LEVELS), LEVELS)
            far_part = decoded(far_in[at, :], far_unit[pl.ds(row, 1), :])
            total = mine[at, :] + decoded(near_in[at, :], near_unit[pl.ds(row, 1), :])
            total += jnp.where(has_far, far_part, 0.0)
            if j < shards - 1:
                code, unit = coded(total)
                z_out[j, to, :] = code
                z_unit_out[j, pl.ds(i, 1), :] = unit
            else:
                mine[at, :] = total

        if j < shards - 1:
            first = 2 * shards + 2 + 2 * j
            pair = [
                remote(z_unit_out.at[j], z_unit.at[j], first, (me, turn)),
                remote(z_out.at[j], z_in.at[j], first + 1, (me, turn)),
            ]
            for copy in pair:
                copy.start()
            shares += pair
    for copy in shares:
        copy.wait_recv()

    @pl.loop(0, blocks)
    def _(i):
        at = pl.ds(pl.multiple_of((ev * blocks + i) * LEVELS, LEVELS), LEVELS)
        to = pl.ds(pl.multiple_of(i * LEVELS, LEVELS), LEVELS)
        total = mine[at, :]
        for j in range(shards - 1):
            total += decoded(z_in[j, to, :], z_unit[j, pl.ds(i, 1), :])
        out[to, :] = img[to, :] * total / sens[to, :]

    for copy in shares + near_copies:
        copy.wait_send()

    @pl.when(has_far)
    def _():
        for copy in far_copies:
            copy.wait_send()


def body(
    home, tiles, classes, tof_bins, subset, correction, background, image, sensitivity, system_table
):
    slab, tile = image.shape
    rows, count = tiles.shape
    peers = lax.axis_size("ax")
    shards = lax.axis_size("ev")
    cap = 4 * rows // peers
    group = math.gcd(cap, GROUP)
    me = lax.axis_index("ax")
    odd, _, across = neighbours(me)
    has_far = jnp.logical_and(across >= 0, across < peers)
    vm = pl.BlockSpec(memory_space=pltpu.VMEM)
    sm = pl.BlockSpec(memory_space=pltpu.SMEM)
    hb = pl.BlockSpec(memory_space=pl.ANY)
    got, places, near, far = pl.pallas_call(
        functools.partial(exchange_kernel, peers, shards),
        out_shape=(
            jax.ShapeDtypeStruct((peers, cap, 4 * tile), jnp.bfloat16),
            jax.ShapeDtypeStruct((peers, 2 * count, cap), jnp.int32),
            jax.ShapeDtypeStruct((slab, tile), jnp.bfloat16),
            jax.ShapeDtypeStruct((slab, tile), jnp.bfloat16),
        ),
        in_specs=[vm] * 7 + [hb],
        out_specs=(hb, hb, hb, hb),
        scratch_shapes=[
            pltpu.VMEM((rows, 4 * tile), jnp.bfloat16),
            pltpu.VMEM((peers, cap, 4 * tile), jnp.bfloat16),
            pltpu.VMEM((peers, 2 * count, cap), jnp.int32),
            pltpu.VMEM((slab // 2, tile), jnp.float32),
            pltpu.VMEM((slab, tile), jnp.float32),
            pltpu.VMEM((slab // 2, tile), jnp.bfloat16),
            pltpu.VMEM((slab, tile), jnp.bfloat16),
            pltpu.SemaphoreType.DMA((2 * peers + shards,)),
            pltpu.SemaphoreType.DMA((2 * peers + shards,)),
            pltpu.SemaphoreType.DMA((4,)),
        ],
        compiler_params=pltpu.CompilerParams(
            collective_id=0, has_side_effects=True, vmem_limit_bytes=VMEM_LIMIT
        ),
    )(home.T, tiles.T, classes.T, tof_bins, subset, correction, background, image)
    got = got.reshape(peers * cap, 4 * tile)
    flags = jnp.stack([odd, has_far.astype(jnp.int32)])
    codes, units, own = pl.pallas_call(
        functools.partial(project_kernel, peers, cap, group),
        out_shape=(
            jax.ShapeDtypeStruct((2, slab, tile), jnp.int16),
            jax.ShapeDtypeStruct((2, slab // LEVELS, tile), jnp.float32),
            jax.ShapeDtypeStruct((slab, tile), jnp.float32),
        ),
        in_specs=[sm, sm, vm, hb, hb, hb, vm],
        out_specs=(hb, hb, hb),
        scratch_shapes=[
            pltpu.VMEM((3 * slab, tile), jnp.float32),
            pltpu.VMEM((2 * slab, tile), jnp.float32),
            pltpu.VMEM((2 * slab, tile), jnp.float32),
            pltpu.VMEM((2 * slab, tile), jnp.float32),
            pltpu.VMEM((2 * slab, tile), jnp.float32),
            pltpu.VMEM((2, slab, tile), jnp.bfloat16),
            pltpu.VMEM((2, slab, tile), jnp.int16),
            pltpu.VMEM((2, slab // LEVELS, tile), jnp.float32),
            pltpu.VMEM((count * group, tile), jnp.float32),
            pltpu.VMEM((count * group, tile), jnp.float32),
            pltpu.SemaphoreType.DMA((3,)),
        ],
        compiler_params=pltpu.CompilerParams(vmem_limit_bytes=VMEM_LIMIT),
        cost_estimate=pl.CostEstimate(flops=1 << 34, bytes_accessed=32 << 20, transcendentals=0),
    )(flags, places, got, image, near, far, system_table)
    quarter = slab // shards
    copies = 4 * shards
    return pl.pallas_call(
        functools.partial(combine_kernel, peers, shards),
        out_shape=jax.ShapeDtypeStruct((quarter, tile), jnp.float32),
        in_specs=[hb, hb, hb, hb, vm],
        out_specs=vm,
        scratch_shapes=[
            pltpu.VMEM((slab, tile), jnp.int16),
            pltpu.VMEM((slab, tile), jnp.int16),
            pltpu.VMEM((slab // LEVELS, tile), jnp.float32),
            pltpu.VMEM((slab // LEVELS, tile), jnp.float32),
            pltpu.VMEM((shards - 1, quarter, tile), jnp.int16),
            pltpu.VMEM((shards - 1, quarter // LEVELS, tile), jnp.float32),
            pltpu.VMEM((shards - 1, quarter, tile), jnp.int16),
            pltpu.VMEM((shards - 1, quarter // LEVELS, tile), jnp.float32),
            pltpu.VMEM((slab, tile), jnp.float32),
            pltpu.VMEM((quarter, tile), jnp.float32),
            pltpu.SemaphoreType.DMA((copies,)),
            pltpu.SemaphoreType.DMA((copies,)),
            pltpu.SemaphoreType.DMA((2,)),
        ],
        compiler_params=pltpu.CompilerParams(
            collective_id=1, has_side_effects=True, vmem_limit_bytes=VMEM_LIMIT
        ),
    )(codes, units, own, image, sensitivity)


def solution(mesh):
    split = P(("ax", "ev"), None)
    placed = (split,) * 7 + (P("ax", None), split, P())
    return jax.shard_map(body, mesh=mesh, in_specs=placed, out_specs=split, check_vma=False)
```
